256 devices in a mesh: row: 16 (over z_hi, x, core), col: 16 (over y, z_lo).
Axes of the slice: x: 4, y: 4, z: 8 (z_hi: 2, z_lo: 4; z = z_hi * 4 + z_lo), core: 2. Of those that a mesh axis runs over, the one named last changes fastest.
Arguments:
- latent: bfloat16 [1280, 64, 128], P('row', 'col'), may hold values from -100 to 100
- stale_act: bfloat16 [1280, 64, 128], P('row', 'col'), may hold values from -6 to 6
- stale_kv: bfloat16 [2, 1280, 64, 128], P(None, None, 'col'), may hold values from -400 to 400
- gn_gain: float32 [1280], P('row'), may hold values from 0.5 to 1.5
- gn_bias: float32 [1280], P('row'), may hold values from -3 to 3
- temb: float32 [1280], P('row'), may hold values from -4 to 4
- conv_w: bfloat16 [3, 3, 1280, 1280], P(None, None, 'row'), may hold values from -0.3125 to 0.3125
- w_qkv: bfloat16 [1280, 3, 1280], P('row'), may hold values from -0.15625 to 0.15625
Outputs:
- hidden: bfloat16 [1280, 64, 128], P('row', 'col')
- attn: bfloat16 [512, 64, 320], P('row', 'col')
The draws below stay inside these ranges and needn't reach their ends.
All inputs are finite; a program needn't handle non-finite values.
Results may differ from the reference program's by a relative error of at most 0.024.
Values may be sent and summed in bfloat16 or wider, within the bound.
A program may use at most 128 MiB of HBM per device.

```python
import jax
import jax.numpy as jnp
from jax import lax

D = 1280
HEADS = 20
HEAD = 64
HGROUPS = 4
GROUPS = 32
NH = 128
CW = 4
W = 64


def block_field(values):
    return jnp.repeat(jnp.repeat(values, D // GROUPS, axis=0), CW, axis=1)[:, :, None]


def draw_latent(key, part):
    key = jax.random.fold_in(key, 11)
    noise_key, level_key, offset_key = jax.random.split(key, 3)
    band_count = W // CW
    column = jnp.arange(W, dtype=jnp.float32) / max(W - 1, 1)
    channel = jnp.arange(D, dtype=jnp.float32) / max(D - 1, 1)
    ramp = (1.0 + channel)[:, None, None] * (1.0 + 9.0 * column)[None, :, None]
    level = jnp.exp(jax.random.uniform(level_key, (GROUPS, band_count), jnp.float32, -1.0, 1.0))
    offset = jax.random.uniform(offset_key, (GROUPS, band_count), jnp.float32, -2.0, 2.0)
    base = jnp.clip(jax.random.normal(noise_key, (D, W, NH), jnp.float32), -4.0, 4.0) + 1.0
    value = 0.2 * base * ramp * block_field(level) + block_field(offset)
    return jnp.clip(value, -100.0, 100.0).astype(jnp.bfloat16)


def draw_stale_kv(key, part):
    key = jax.random.fold_in(key, 12)
    first = jax.random.fold_in(key, 0)
    base = jnp.clip(jax.random.normal(first, (2, D, W, NH), jnp.float32), -5.0, 5.0)
    return base.astype(jnp.bfloat16)


def shard_levels(rng, dims, pieces, least, high):
    loudness, own = 1.0, jax.random.fold_in(rng, 6)
    for dim, parts in pieces:
        steps = jnp.exp(jax.random.uniform(jax.random.fold_in(own, dim), (parts,), jnp.float32, least / len(pieces), high / len(pieces)))
        loudness = loudness * jnp.repeat(steps, dims[dim] // parts).reshape([-1 if axis == dim else 1 for axis in range(len(dims))])
    return loudness


def bell_draw(stream_key, shape, scale, reach, pieces=(), kind=jnp.bfloat16):
    values = jax.random.normal(stream_key, shape, jnp.float32) * scale
    if len(pieces) > 0:
        values = shard_levels(stream_key, shape, pieces, -0.22, 0.18) * values
    return jnp.clip(values, min=-reach, max=reach).astype(kind)


def setup_inputs(seed: int = 0) -> dict:
    splits = jax.random.split(jax.random.key(seed), 9)
    latent = draw_latent(jax.random.fold_in(splits[8], 71), 0)
    stale_act = bell_draw(splits[1], (D, W, NH), 1.0, 6.0, ((0, 16), (1, 16)))
    stale_kv = draw_stale_kv(jax.random.fold_in(splits[8], 71), 0)
    gn_gain = jnp.clip(0.5 + 1.0 * jax.random.uniform(splits[3], (D,), jnp.float32) ** shard_levels(splits[3], (D,), ((0, 16),), -0.2, 0.2), 0.5, 1.5)
    gn_bias = bell_draw(splits[4], (D,), 0.5, 3.0, ((0, 16),), jnp.float32)
    temb = bell_draw(splits[5], (D,), 1.0, 4.0, ((0, 16),), jnp.float32)
    conv_w = bell_draw(splits[6], (3, 3, D, D), (D // 4) ** -0.5, 0.3125, ((2, 16),))
    w_qkv = bell_draw(splits[7], (D, 3, D), D ** -0.5, 0.15625, ((0, 16),))
    return dict(latent=latent, stale_act=stale_act, stale_kv=stale_kv, gn_gain=gn_gain, gn_bias=gn_bias, temb=temb, conv_w=conv_w, w_qkv=w_qkv)


EPS = 1e-05

def reference(latent, stale_act, stale_kv, gn_gain, gn_bias, temb, conv_w, w_qkv):
    band_tokens = CW * NH
    bands = W // CW
    xf = latent.astype(jnp.float32)
    grouped = xf.reshape(GROUPS, D // GROUPS, W * NH)
    gmean = lax.optimization_barrier(jnp.mean(grouped, axis=(1, 2), keepdims=True))
    gvar = lax.optimization_barrier(jnp.mean((grouped - gmean) ** 2, axis=(1, 2), keepdims=True))
    normed = ((grouped - gmean) * lax.rsqrt(gvar + EPS)).reshape(D, W, NH)
    act = jax.nn.silu(normed * gn_gain[:, None, None] + gn_bias[:, None, None]).astype(jnp.bfloat16)

    def conv_band(band):
        first = band * CW
        inner = lax.dynamic_slice_in_dim(act, first, CW, 1)
        left = lax.dynamic_slice_in_dim(stale_act, jnp.maximum(first - 1, 0).astype(jnp.int32), 1, 1)
        left = jnp.where(band > 0, left, jnp.zeros_like(left))
        right = lax.dynamic_slice_in_dim(stale_act, jnp.minimum(first + CW, W - 1).astype(jnp.int32), 1, 1)
        right = jnp.where(band < bands - 1, right, jnp.zeros_like(right))
        block = jnp.concatenate([left, inner, right], axis=1)
        block = jnp.pad(block, ((0, 0), (0, 0), (1, 1)))
        total = jnp.zeros((D, band_tokens), jnp.float32)
        for shift_w in range(3):
            for shift_h in range(3):
                piece = block[:, shift_w:shift_w + CW, shift_h:shift_h + NH].reshape(D, band_tokens)
                total = total + jnp.dot(conv_w[shift_w, shift_h].T, piece, preferred_element_type=jnp.float32)
        return total
    conv = lax.map(conv_band, jnp.arange(bands, dtype=jnp.int32))
    conv = conv.transpose(1, 0, 2).reshape(D, W, NH)
    hidden = (xf + conv + temb[:, None, None]).astype(jnp.bfloat16)
    flat = hidden.reshape(D, W * NH)
    hfloat = flat.astype(jnp.float32)
    mu = lax.optimization_barrier(jnp.mean(hfloat, axis=0))
    rstd = lax.rsqrt(lax.optimization_barrier(jnp.mean(hfloat * hfloat, axis=0)) - mu * mu + EPS)
    wmat = w_qkv.reshape(D, 3 * D)
    proj = jnp.dot(wmat.T, flat, preferred_element_type=jnp.float32)
    colsum = lax.optimization_barrier(jnp.sum(wmat.astype(jnp.float32), axis=0))
    qkv = ((proj - colsum[:, None] * mu[None, :]) * rstd[None, :]).astype(jnp.bfloat16)
    qkv = qkv.reshape(3, HEADS, HEAD, W * NH)
    stale = stale_kv.reshape(2, HEADS, HEAD, W * NH)
    band_of = jnp.arange(W * NH, dtype=jnp.int32) // band_tokens
    scale = HEAD ** (-0.5)

    def attend_band(band):
        own = (band_of == band)[None, :]

        def attend_head(head):
            query = lax.dynamic_slice_in_dim(qkv[0, head], (band * band_tokens).astype(jnp.int32), band_tokens, 1)
            keys = jnp.where(own, qkv[1, head], stale[0, head])
            values = jnp.where(own, qkv[2, head], stale[1, head])
            scores = jnp.dot(query.T, keys, preferred_element_type=jnp.float32) * scale
            weights = jax.nn.softmax(scores, axis=1).astype(jnp.bfloat16)
            return jnp.dot(values, weights.T, preferred_element_type=jnp.float32)
        return lax.map(attend_head, jnp.arange(HEADS, dtype=jnp.int32))
    result = lax.map(attend_band, jnp.arange(bands, dtype=jnp.int32))
    attn = result.transpose(1, 2, 0, 3).reshape(D, W, NH).astype(jnp.bfloat16)
    attn = attn.reshape(HGROUPS, D // HGROUPS, W, NH).transpose(0, 3, 2, 1).reshape(HGROUPS * NH, W, D // HGROUPS)
    return (hidden, attn)
```

```python
import itertools
import math

import jax
import jax.numpy as jnp
from jax import lax
from jax.experimental import pallas as pl
from jax.experimental.pallas import tpu as pltpu
from jax.sharding import PartitionSpec as P

D = 1280
HEAD = 64
HGROUPS = 4
GROUPS = 32
EPS = 1e-05

F32 = jnp.float32
BF16 = jnp.bfloat16
MESH = pl.DeviceIdType.MESH

CH = 80
GC = 320
NHEAD = 5
COLS = 4
ROWS = 128
TOK = COLS * ROWS
QT = 128
NSEM = 80


def dot(a, b, ca, cb):
    return lax.dot_general(a, b, (((ca,), (cb,)), ((), ())), preferred_element_type=F32)


def as_column(row):
    n = row.shape[1]
    r = lax.broadcasted_iota(jnp.int32, (n, n), 0)
    c = lax.broadcasted_iota(jnp.int32, (n, n), 1)
    return jnp.sum(jnp.where(r == c, jnp.broadcast_to(row, (n, n)), 0.0), axis=1, keepdims=True)


def kernel(
    lat_ref, edge_ref, kv_hbm, gain_ref, bias_ref, temb_ref, cw_hbm, w_ref,
    hid_ref, attn_ref,
    cw, wsrc, wt, wtsib, x3, x3sib, halo, st_a, st_all, pb, rx, zs, zr,
    hall, wz, wg, kb, kf, qx, qpeer, oown, oret, oback, lret, lback, lses,
    ss, rs, ls,
):
    row = lax.axis_index("row")
    col = lax.axis_index("col")
    zh, x, k = row // 8, (row // 2) % 4, row % 2
    y, zl = col // 4, col % 4
    group = row // 4
    part = row % 4
    ids = itertools.count()

    def at_row(zh_, x_, k_):
        return zh_ * 8 + x_ * 2 + k_

    def dev(r, c):
        return (r, c)

    sib = dev(at_row(zh, x, 1 - k), col)
    wpeer = (at_row(1 - zh, x, k), y * 4 + 3 - zl)
    zpeer = dev(at_row(1 - zh, x, k), col)
    xs = {d: (x + d) % 4 for d in (1, 2, 3)}
    xpeer = {d: dev(at_row(zh, xs[d], k), col) for d in (1, 2, 3)}
    ypeer = {d: dev(row, ((y + d) % 4) * 4 + zl) for d in (1, 2, 3)}
    lpeer = {d: dev(row, y * 4 + (zl + d) % 4) for d in (1, 2, 3)}
    nxt = dev(row, (col + 1) % 16)
    prv = dev(row, (col + 15) % 16)
    flip = zl + 1 - 2 * (zl % 2)
    near = dev(row, y * 4 + flip)
    qpartner = lpeer[2]
    others = {
        (dy, dz): dev(row, ((y + dy) % 4) * 4 + (zl + dz) % 4)
        for dy in range(4) for dz in range(4) if dy or dz
    }
    r_z = at_row(1 - zh, x, k)

    started = []

    def rcopy(src, dst, to):
        i = next(ids)
        cp = pltpu.make_async_remote_copy(
            src_ref=src, dst_ref=dst, send_sem=ss.at[i], recv_sem=rs.at[i],
            device_id=to, device_id_type=MESH,
        )
        cp.start()
        started.append(cp)
        return cp

    lc_w = pltpu.make_async_copy(cw_hbm, cw, ls.at[0])
    lc_w.start()
    lc_kv = pltpu.make_async_copy(kv_hbm, kb.at[:, 0], ls.at[1])
    lc_kv.start()

    bar = pltpu.get_barrier_semaphore()
    peers = [sib, zpeer, wpeer, *xpeer.values(), *others.values(), nxt, prv]
    for p in peers:
        pl.semaphore_signal(bar, inc=1, device_id=p, device_id_type=MESH)

    for i in range(3):
        part_w = w_ref[i]
        for g in range(HGROUPS):
            wsrc[g, :, i * GC:(i + 1) * GC] = part_w[:, g * GC:(g + 1) * GC]
    lc_own = pltpu.make_async_copy(wsrc.at[group], wg.at[row], ls.at[2])
    lc_own.start()

    xf = lat_ref[...].astype(F32)
    n_loc = 40 * TOK
    halves = [xf[0:40], xf[40:80]]
    means = [jnp.sum(jnp.sum(h, axis=1, keepdims=True), axis=0, keepdims=True) / n_loc for h in halves]
    m2s = [
        jnp.sum(jnp.sum((h - m) * (h - m), axis=1, keepdims=True), axis=0, keepdims=True)
        for h, m in zip(halves, means)
    ]
    rid = lax.broadcasted_iota(jnp.int32, (8, 128), 0)
    tile = jnp.zeros((8, 128), F32)
    for i, v in enumerate(means + m2s):
        tile = jnp.where(rid == i, jnp.broadcast_to(v, (8, 128)), tile)
    st_a[...] = tile

    pl.semaphore_wait(bar, len(peers))

    c_st = [
        rcopy(st_a, st_all.at[dy * 4 + dz - 1], to) for (dy, dz), to in others.items()
    ]
    c_halo_n = rcopy(edge_ref.at[1], halo.at[0], nxt)
    c_halo_p = rcopy(edge_ref.at[0], halo.at[1], prv)

    c_wx = {d: rcopy(wsrc.at[zh * 2 + xs[d] // 2], wg.at[row], xpeer[d]) for d in (1, 2, 3)}
    c_ws = rcopy(wsrc.at[group], wg.at[row], sib)
    lc_w.wait()
    eye = (
        lax.broadcasted_iota(jnp.int32, (128, 128), 0) == lax.broadcasted_iota(jnp.int32, (128, 128), 1)
    ).astype(BF16)

    def flip_weights(a):
        for half in range(2):
            blocks = [
                dot(eye, cw[a, :, (half * 5 + i) * 128:(half * 5 + i + 1) * 128], 1, 1).astype(BF16)
                for i in range(5)
            ]
            wt[a, half] = jnp.concatenate(blocks, axis=0).reshape(4, 2, CH, 240)

    flip_weights(0)

    flip_weights(1)
    flip_weights(2)
    c_wt = rcopy(wt.at[:, :, :, 1 - k], wtsib, sib)

    lane = lax.broadcasted_iota(jnp.int32, (CH, ROWS), 1)

    def shifts(colv):
        left = jnp.where(lane == 0, 0.0, pltpu.roll(colv, 1, axis=1))
        right = jnp.where(lane == ROWS - 1, 0.0, pltpu.roll(colv, ROWS - 1, axis=1))
        return [left.astype(BF16), colv.astype(BF16), right.astype(BF16)]

    def put_column(slot, colv):
        for c, v in enumerate(shifts(colv)):
            x3[c * CH:(c + 1) * CH, slot * ROWS:(slot + 1) * ROWS] = v

    gain = as_column(gain_ref[...])
    bias = as_column(bias_ref[...])
    temb = as_column(temb_ref[...])

    c_halo_n.wait_recv()
    c_halo_p.wait_recv()
    put_column(0, jnp.where(col > 0, halo[0].astype(F32), 0.0))
    put_column(5, jnp.where(col < 15, halo[1].astype(F32), 0.0))

    for c in c_st:
        c.wait_recv()
    tiles = [tile] + [st_all[i] for i in range(15)]
    gmean = sum(t[0:2] for t in tiles) / 16.0
    gm2 = sum(t[2:4] for t in tiles)
    for t in tiles:
        dlt = t[0:2] - gmean
        gm2 = gm2 + float(n_loc) * dlt * dlt
    ginv = lax.rsqrt(gm2 / float(16 * n_loc) + EPS)
    c_near = rcopy(kv_hbm.at[k], kb.at[k, 4], near)
    c_wz = rcopy(wsrc.at[pl.ds(2 * (1 - zh), 2)], wz, wpeer)
    c_kvy = {d: rcopy(kv_hbm.at[k], kb.at[k, d], ypeer[d]) for d in (1, 2, 3)}
    mean_c = jnp.concatenate(
        [jnp.broadcast_to(gmean[0:1], (40, 128)), jnp.broadcast_to(gmean[1:2], (40, 128))], axis=0
    )
    inv_c = jnp.concatenate(
        [jnp.broadcast_to(ginv[0:1], (40, 128)), jnp.broadcast_to(ginv[1:2], (40, 128))], axis=0
    )
    for w in range(COLS):
        v = (xf[:, w * ROWS:(w + 1) * ROWS] - mean_c) * inv_c * gain + bias
        act = v / (1.0 + jnp.exp(-v))
        put_column(1 + w, act.astype(BF16).astype(F32))
    c_x3 = rcopy(x3, x3sib, sib)

    c_wt.wait_recv()
    c_x3.wait_recv()
    c_rx = []
    for half in range(2):
        zz = (1 - zh) if half == 0 else zh
        acc = jnp.zeros((4 * CH, TOK), F32)
        for a in range(3):
            acc = acc + dot(
                wt[a, zz, :, k].reshape(4 * CH, 240), x3[:, a * ROWS:a * ROWS + TOK], 1, 0
            )
        for a in range(3):
            acc = acc + dot(
                wtsib[a, zz].reshape(4 * CH, 240), x3sib[:, a * ROWS:a * ROWS + TOK], 1, 0
            )
        pb[half] = acc.astype(BF16).reshape(4, CH, TOK)
        c_rx.append([rcopy(pb.at[half, xs[d]], rx.at[half, d - 1], xpeer[d]) for d in (1, 2, 3)])

    def keys_second():
        c_near.wait_recv()
        ks = [rcopy(kb.at[k, 4], kb.at[k, 4], sib)]
        return {d: rcopy(kb.at[k, 4], kb.at[k, 4 + d], ypeer[d]) for d in (1, 2, 3)}, ks

    def weights_second():
        mine = x // 2
        c_wz.wait_recv()
        lc = pltpu.make_async_copy(wz.at[mine], wg.at[r_z], ls.at[3])
        lc.start()
        cx = {d: rcopy(wz.at[xs[d] // 2], wg.at[r_z], xpeer[d]) for d in (1, 2, 3)}
        return lc, cx, rcopy(wz.at[mine], wg.at[r_z], sib)

    sums = []
    for half in range(2):
        for c in c_rx[half]:
            c.wait_recv()
        total = pb[half, x].astype(F32)
        for d in range(3):
            total = total + rx[half, d].astype(F32)
        if half == 0:
            zs[...] = total.astype(BF16)
            c_zr = rcopy(zs, zr, zpeer)
        sums.append(total)

    c_kvy2, c_ks = keys_second()
    lc_z, c_wx2, c_ws2 = weights_second()

    c_zr.wait_recv()
    hid = (xf + (sums[1] + zr[...].astype(F32)) + temb).astype(BF16)
    hid_ref[...] = hid
    hall[row] = hid

    c_hz = rcopy(hall.at[row], hall.at[row], zpeer)
    c_hx = {d: rcopy(hall.at[row], hall.at[row], xpeer[d]) for d in (1, 2, 3)}
    c_hs = [rcopy(hall.at[row], hall.at[row], sib)]
    c_hz.wait_recv()
    c_hx2 = {d: rcopy(hall.at[r_z], hall.at[r_z], xpeer[d]) for d in (1, 2, 3)}
    c_hs.append(rcopy(hall.at[r_z], hall.at[r_z], sib))

    w_fwd = []
    for d in (1, 2, 3):
        src = at_row(zh, (x + 4 - d) % 4, k)
        c_wx[d].wait_recv()
        w_fwd.append(rcopy(wg.at[src], wg.at[src], sib))
        c_kvy[d].wait_recv()
        c_ks.append(rcopy(kb.at[k, d], kb.at[k, d], sib))
    for leg, cs in ((0, c_hx), (1, c_hx2)):
        for d in (1, 2, 3):
            src = at_row(zh if leg == 0 else 1 - zh, (x + 4 - d) % 4, k)
            cs[d].wait_recv()
            c_hs.append(rcopy(hall.at[src], hall.at[src], sib))
    for d in (1, 2, 3):
        src = at_row(1 - zh, (x + 4 - d) % 4, k)
        c_wx2[d].wait_recv()
        w_fwd.append(rcopy(wg.at[src], wg.at[src], sib))

    c_kfwd = []
    for d in (1, 2, 3):
        c_kvy2[d].wait_recv()
        c_kfwd.append(rcopy(kb.at[k, 4 + d], kb.at[k, 4 + d], sib))

    lc_own.wait()
    lc_z.wait()
    for c in [c_ws, c_ws2, *w_fwd]:
        c.wait_recv()
    wfull = wg[...].reshape(D, 3 * GC)
    colsum = dot(wfull, jnp.ones((D, 128), BF16), 0, 0)
    for c in c_hs:
        c.wait_recv()

    hfull = hall[...].reshape(D, TOK)
    hf = hfull.astype(F32)
    mu = jnp.sum(hf, axis=0, keepdims=True) / D
    nvar = jnp.sum(hf * hf, axis=0, keepdims=True) / D - mu * mu
    rstd = lax.rsqrt(nvar + EPS)
    proj = dot(wfull, hfull, 0, 0)
    qkv = (proj - colsum[:, 0:1] * mu) * rstd
    qcm = (qkv[0:GC] * (HEAD ** -0.5 * math.log2(math.e))).astype(BF16)
    kf[0] = qkv[GC:2 * GC].astype(BF16)
    kf[1] = qkv[2 * GC:].astype(BF16)

    qi = lax.broadcasted_iota(jnp.int32, (QT, TOK), 0)
    ti = lax.broadcasted_iota(jnp.int32, (QT, TOK), 1)
    pick = (ti == (qi & 3) * ROWS + part * 32 + (qi >> 2)).astype(BF16)
    qtm = dot(pick, qcm, 1, 1).astype(BF16)
    qx[...] = qtm
    c_q = rcopy(qx, qpeer, qpartner)

    lc_kv.wait()
    for c in c_ks + c_kfwd:
        c.wait_recv()

    def head_rows(h):
        return pl.ds(h * HEAD, HEAD)

    def keys_of(h, own):
        first = kf[0, head_rows(h), :] if own else kb[0, 0, head_rows(h), :]
        return [first] + [kb[0, i, head_rows(h), :] for i in range(1, 8)]

    def values_of(h, own):
        first = kf[1, head_rows(h), :] if own else kb[1, 0, head_rows(h), :]
        return [first] + [kb[1, i, head_rows(h), :] for i in range(1, 8)]

    def weigh(scores, best, values):
        out = jnp.zeros((QT, HEAD + 16), F32)
        for s, v in zip(scores, values):
            p = jnp.exp2(s - best).astype(BF16)
            out = out + dot(p, jnp.concatenate([v, jnp.ones((16, TOK), BF16)], axis=0), 1, 1)
        norm = out[:, HEAD:HEAD + 1]
        return out[:, 0:HEAD] / norm, best + jnp.log2(norm)

    diag = lax.broadcasted_iota(jnp.int32, (QT, QT), 0) == lax.broadcasted_iota(jnp.int32, (QT, QT), 1)
    c_o = []

    def finish(h, own, scores, best):
        o, lse = weigh(scores, best, values_of(h, own))
        if own:
            oown[h] = o
            lses[h] = jnp.broadcast_to(lse, (QT, 128))
            return
        oret[h // 2, :, (h % 2) * HEAD:(h % 2 + 1) * HEAD] = o.astype(BF16)
        lret[h:h + 1] = jnp.sum(
            jnp.where(diag, jnp.broadcast_to(lse, (QT, QT)), 0.0), axis=0, keepdims=True
        )
        if h % 2 == 1:
            c_o.append(rcopy(oret.at[h // 2], oback.at[h // 2], qpartner))

    lret[...] = jnp.zeros((8, 128), F32)
    oret[2, :, HEAD:128] = jnp.zeros((QT, HEAD), BF16)
    held = None
    for own in (True, False):
        if not own:
            c_q.wait_recv()
        q_all = qtm if own else qpeer[...]
        for h in range(NHEAD):
            q = q_all[:, h * HEAD:(h + 1) * HEAD]
            scores = [dot(q, kk, 1, 0) for kk in keys_of(h, own)]
            top = scores[0]
            for sc in scores[1:]:
                top = jnp.maximum(top, sc)
            best = jnp.max(top, axis=1, keepdims=True)
            if held is not None:
                finish(*held)
            held = (h, own, scores, best)
    finish(*held)
    c_o.append(rcopy(oret.at[2], oback.at[2], qpartner))
    c_o.append(rcopy(lret, lback, qpartner))
    for c in c_o:
        c.wait_recv()

    outs = []
    for h in range(NHEAD):
        o1 = oback[h // 2, :, (h % 2) * HEAD:(h % 2 + 1) * HEAD].astype(F32)
        lse1 = as_column(lback[h:h + 1])
        lse0 = lses[h][:, 0:1]
        top = jnp.maximum(lse0, lse1)
        w0 = jnp.exp2(lse0 - top)
        w1 = jnp.exp2(lse1 - top)
        outs.append((oown[h] * w0 + o1 * w1) / (w0 + w1))
    attn_ref[...] = jnp.concatenate(outs, axis=1).astype(BF16)

    for c in started:
        c.wait_send()


def on_device(latent, stale_act, stale_kv, gn_gain, gn_bias, temb, conv_w, w_qkv):
    group = lax.axis_index("row") // 4
    lat = latent.reshape(CH, TOK)
    edges = jnp.stack([stale_act[:, 0], stale_act[:, COLS - 1]])
    kv = lax.dynamic_slice_in_dim(stale_kv, group * GC, GC, 1).reshape(2, GC, TOK)
    vm = pl.BlockSpec(memory_space=pltpu.VMEM)
    hbm = pl.BlockSpec(memory_space=pl.ANY)
    scratch = [
        pltpu.VMEM((3, 240, D), BF16),
        pltpu.VMEM((HGROUPS, CH, 3 * GC), BF16),
        pltpu.VMEM((3, 2, 4, 2, CH, 240), BF16),
        pltpu.VMEM((3, 2, 4, CH, 240), BF16),
        pltpu.VMEM((240, 6 * ROWS), BF16),
        pltpu.VMEM((240, 6 * ROWS), BF16),
        pltpu.VMEM((2, CH, ROWS), BF16),
        pltpu.VMEM((8, 128), F32),
        pltpu.VMEM((15, 8, 128), F32),
        pltpu.VMEM((2, 4, CH, TOK), BF16),
        pltpu.VMEM((2, 3, CH, TOK), BF16),
        pltpu.VMEM((CH, TOK), BF16),
        pltpu.VMEM((CH, TOK), BF16),
        pltpu.VMEM((16, CH, TOK), BF16),
        pltpu.VMEM((2, CH, 3 * GC), BF16),
        pltpu.VMEM((16, CH, 3 * GC), BF16),
        pltpu.VMEM((2, 8, GC, TOK), BF16),
        pltpu.VMEM((2, GC, TOK), BF16),
        pltpu.VMEM((QT, GC), BF16),
        pltpu.VMEM((QT, GC), BF16),
        pltpu.VMEM((NHEAD, QT, HEAD), F32),
        pltpu.VMEM((3, QT, 128), BF16),
        pltpu.VMEM((3, QT, 128), BF16),
        pltpu.VMEM((8, 128), F32),
        pltpu.VMEM((8, 128), F32),
        pltpu.VMEM((NHEAD, QT, 128), F32),
        pltpu.SemaphoreType.DMA((NSEM,)),
        pltpu.SemaphoreType.DMA((NSEM,)),
        pltpu.SemaphoreType.DMA((4,)),
    ]
    hid, attn = pl.pallas_call(
        kernel,
        out_shape=(
            jax.ShapeDtypeStruct((CH, TOK), BF16),
            jax.ShapeDtypeStruct((QT, GC), BF16),
        ),
        in_specs=[vm, vm, hbm, vm, vm, vm, hbm, vm],
        out_specs=(vm, vm),
        scratch_shapes=scratch,
        compiler_params=pltpu.CompilerParams(
            collective_id=0, has_side_effects=True, vmem_limit_bytes=56 << 20
        ),
    )(
        lat, edges, kv, gn_gain.reshape(1, CH), gn_bias.reshape(1, CH), temb.reshape(1, CH),
        conv_w.reshape(3, 240, D), w_qkv.transpose(1, 0, 2),
    )
    return hid.reshape(CH, COLS, ROWS), attn.reshape(32, COLS, GC)


def solution(mesh):
    return jax.shard_map(
        on_device,
        mesh=mesh,
        in_specs=(
            P("row", "col", None),
            P("row", "col", None),
            P(None, None, "col", None),
            P("row"),
            P("row"),
            P("row"),
            P(None, None, "row", None),
            P("row", None, None),
        ),
        out_specs=(P("row", "col", None), P("row", "col", None)),
        check_vma=False,
    )
```

```python
import itertools

import jax
import jax.numpy as jnp
from jax import lax
from jax.experimental import pallas as pl
from jax.experimental.pallas import tpu as pltpu
from jax.sharding import PartitionSpec as P

D = 1280
HEAD = 64
HGROUPS = 4
GROUPS = 32
EPS = 1e-05

F32 = jnp.float32
BF16 = jnp.bfloat16
MESH = pl.DeviceIdType.MESH

CH = 80
GC = 320
NHEAD = 5
COLS = 4
ROWS = 128
TOK = COLS * ROWS
QT = 128
NSEM = 128
HT = TOK // 2


def dot(a, b, ca, cb):
    return lax.dot_general(a, b, (((ca,), (cb,)), ((), ())), preferred_element_type=F32)


def as_column(row):
    n = row.shape[1]
    r = lax.broadcasted_iota(jnp.int32, (n, n), 0)
    c = lax.broadcasted_iota(jnp.int32, (n, n), 1)
    return jnp.sum(jnp.where(r == c, jnp.broadcast_to(row, (n, n)), 0.0), axis=1, keepdims=True)


def kernel(
    lat_ref, edge_ref, kv_hbm, gain_ref, bias_ref, temb_ref, cw_hbm, w_ref,
    hid_ref, attn_ref,
    cw, wsrc, wt, wtsib, x3, x3sib, halo, st_a, st_all, pb, rx, zs, zr,
    hall, wz, wg, kb, kf, qx, qpeer, oown, oret, oback, lret, lback, lses,
    ss, rs, ls,
):
    row = lax.axis_index("row")
    col = lax.axis_index("col")
    zh, x, k = row // 8, (row // 2) % 4, row % 2
    y, zl = col // 4, col % 4
    group = row // 4
    part = row % 4
    ids = itertools.count()

    def at_row(zh_, x_, k_):
        return zh_ * 8 + x_ * 2 + k_

    def dev(r, c):
        return (r, c)

    sib = dev(at_row(zh, x, 1 - k), col)
    wpeer = (at_row(1 - zh, x, k), y * 4 + 3 - zl)
    zpeer = dev(at_row(1 - zh, x, k), col)
    xs = {d: (x + d) % 4 for d in (1, 2, 3)}
    xpeer = {d: dev(at_row(zh, xs[d], k), col) for d in (1, 2, 3)}
    ypeer = {d: dev(row, ((y + d) % 4) * 4 + zl) for d in (1, 2, 3)}
    lpeer = {d: dev(row, y * 4 + (zl + d) % 4) for d in (1, 2, 3)}
    nxt = dev(row, (col + 1) % 16)
    prv = dev(row, (col + 15) % 16)
    flip = zl + 1 - 2 * (zl % 2)
    near = lpeer[2]
    qpartner = dev(row, y * 4 + flip)
    others = {
        (dy, dz): dev(row, ((y + dy) % 4) * 4 + (zl + dz) % 4)
        for dy in range(4) for dz in range(4) if dy or dz
    }
    r_z = at_row(1 - zh, x, k)

    started = []

    def rcopy(src, dst, to):
        i = next(ids)
        cp = pltpu.make_async_remote_copy(
            src_ref=src, dst_ref=dst, send_sem=ss.at[i], recv_sem=rs.at[i],
            device_id=to, device_id_type=MESH,
        )
        cp.start()
        started.append(cp)
        return cp

    lc_w = pltpu.make_async_copy(cw_hbm, cw, ls.at[0])
    lc_w.start()
    lc_kv = pltpu.make_async_copy(kv_hbm, kb.at[:, 0], ls.at[1])
    lc_kv.start()

    bar = pltpu.get_barrier_semaphore()
    peers = [sib, zpeer, wpeer, *xpeer.values(), *others.values(), nxt, prv]
    for p in peers:
        pl.semaphore_signal(bar, inc=1, device_id=p, device_id_type=MESH)

    for i in range(3):
        part_w = w_ref[i]
        for g in range(HGROUPS):
            wsrc[g, :, i * GC:(i + 1) * GC] = part_w[:, g * GC:(g + 1) * GC]
    lc_own = pltpu.make_async_copy(wsrc.at[group], wg.at[row], ls.at[2])
    lc_own.start()

    xf = lat_ref[...].astype(F32)
    n_loc = 40 * TOK
    halves = [xf[0:40], xf[40:80]]
    means = [jnp.sum(jnp.sum(h, axis=1, keepdims=True), axis=0, keepdims=True) / n_loc for h in halves]
    m2s = [
        jnp.sum(jnp.sum((h - m) * (h - m), axis=1, keepdims=True), axis=0, keepdims=True)
        for h, m in zip(halves, means)
    ]
    rid = lax.broadcasted_iota(jnp.int32, (8, 128), 0)
    tile = jnp.zeros((8, 128), F32)
    for i, v in enumerate(means + m2s):
        tile = jnp.where(rid == i, jnp.broadcast_to(v, (8, 128)), tile)
    st_a[...] = tile

    pl.semaphore_wait(bar, len(peers))

    c_st = [
        rcopy(st_a, st_all.at[dy * 4 + dz - 1], to) for (dy, dz), to in others.items()
    ]
    c_halo_n = rcopy(edge_ref.at[1], halo.at[0], nxt)
    c_halo_p = rcopy(edge_ref.at[0], halo.at[1], prv)

    c_wx = {d: rcopy(wsrc.at[zh * 2 + xs[d] // 2], wg.at[row], xpeer[d]) for d in (1, 2, 3)}
    c_ws = rcopy(wsrc.at[group], wg.at[row], sib)
    lc_w.wait()
    eye = (
        lax.broadcasted_iota(jnp.int32, (128, 128), 0) == lax.broadcasted_iota(jnp.int32, (128, 128), 1)
    ).astype(BF16)

    def flip_weights(a):
        for half in range(2):
            blocks = [
                dot(eye, cw[a, :, (half * 5 + i) * 128:(half * 5 + i + 1) * 128], 1, 1).astype(BF16)
                for i in range(5)
            ]
            wt[a, half] = jnp.concatenate(blocks, axis=0).reshape(4, 2, CH, 240)

    flip_weights(0)

    flip_weights(1)
    flip_weights(2)
    c_wt = rcopy(wt.at[:, :, :, 1 - k], wtsib, sib)

    lane = lax.broadcasted_iota(jnp.int32, (CH, ROWS), 1)

    def shifts(colv):
        left = jnp.where(lane == 0, 0.0, pltpu.roll(colv, 1, axis=1))
        right = jnp.where(lane == ROWS - 1, 0.0, pltpu.roll(colv, ROWS - 1, axis=1))
        return [left.astype(BF16), colv.astype(BF16), right.astype(BF16)]

    def put_column(slot, colv):
        for c, v in enumerate(shifts(colv)):
            x3[c * CH:(c + 1) * CH, slot * ROWS:(slot + 1) * ROWS] = v

    gain = as_column(gain_ref[...])
    bias = as_column(bias_ref[...])
    temb = as_column(temb_ref[...])

    c_halo_n.wait_recv()
    c_halo_p.wait_recv()
    put_column(0, jnp.where(col > 0, halo[0].astype(F32), 0.0))
    put_column(5, jnp.where(col < 15, halo[1].astype(F32), 0.0))

    for c in c_st:
        c.wait_recv()
    tiles = [tile] + [st_all[i] for i in range(15)]
    gmean = sum(t[0:2] for t in tiles) / 16.0
    gm2 = sum(t[2:4] for t in tiles)
    for t in tiles:
        dlt = t[0:2] - gmean
        gm2 = gm2 + float(n_loc) * dlt * dlt
    ginv = lax.rsqrt(gm2 / float(16 * n_loc) + EPS)
    c_wz = rcopy(wsrc.at[pl.ds(2 * (1 - zh), 2)], wz, wpeer)
    c_near = rcopy(kv_hbm.at[k], kb.at[k, 4], near)
    c_kvy = {d: rcopy(kv_hbm.at[k], kb.at[k, d], ypeer[d]) for d in (1, 2, 3)}
    mean_c = jnp.concatenate(
        [jnp.broadcast_to(gmean[0:1], (40, 128)), jnp.broadcast_to(gmean[1:2], (40, 128))], axis=0
    )
    inv_c = jnp.concatenate(
        [jnp.broadcast_to(ginv[0:1], (40, 128)), jnp.broadcast_to(ginv[1:2], (40, 128))], axis=0
    )
    for w in range(COLS):
        v = (xf[:, w * ROWS:(w + 1) * ROWS] - mean_c) * inv_c * gain + bias
        act = v / (1.0 + jnp.exp(-v))
        put_column(1 + w, act.astype(BF16).astype(F32))
    c_x3 = rcopy(x3, x3sib, sib)

    c_wt.wait_recv()
    c_x3.wait_recv()
    c_rx = {}
    for t in range(2):
        for half in range(2):
            zz = (1 - zh) if half == 0 else zh
            acc = jnp.zeros((4 * CH, HT), F32)
            for wv, xv in ((wt.at[:, :, :, k], x3), (wtsib, x3sib)):
                for a in range(3):
                    first = a * ROWS + t * HT
                    acc = acc + dot(
                        wv[a, zz].reshape(4 * CH, 240), xv[:, first:first + HT], 1, 0
                    )
            pb[t, half] = acc.astype(BF16).reshape(4, CH, HT)
            c_rx[t, half] = [
                rcopy(pb.at[t, half, xs[d]], rx.at[t, half, d - 1], xpeer[d]) for d in (1, 2, 3)
            ]

    def keys_second():
        c_near.wait_recv()
        ks = [rcopy(kb.at[k, 4], kb.at[k, 4], sib)]
        return {d: rcopy(kb.at[k, 4], kb.at[k, 4 + d], ypeer[d]) for d in (1, 2, 3)}, ks

    def weights_second():
        mine = x // 2
        c_wz.wait_recv()
        lc = pltpu.make_async_copy(wz.at[mine], wg.at[r_z], ls.at[3])
        lc.start()
        cx = {d: rcopy(wz.at[xs[d] // 2], wg.at[r_z], xpeer[d]) for d in (1, 2, 3)}
        return lc, cx, rcopy(wz.at[mine], wg.at[r_z], sib)

    def collect(t, half):
        total = pb[t, half, x].astype(F32)
        for d in range(3):
            c_rx[t, half][d].wait_recv()
            total = total + rx[t, half, d].astype(F32)
        return total

    def block(r, t):
        return hall.at[r, :, pl.ds(t * HT, HT)]

    def residual(t, own):
        c_zr[t].wait_recv()
        lanes = slice(t * HT, (t + 1) * HT)
        hid = (xf[:, lanes] + (own + zr[t].astype(F32)) + temb).astype(BF16)
        hid_ref[:, lanes] = hid
        hall[row, :, lanes] = hid
        c_hz.append(rcopy(block(row, t), block(row, t), zpeer))
        c_hx[t] = {d: rcopy(block(row, t), block(row, t), xpeer[d]) for d in (1, 2, 3)}
        c_hs.append(rcopy(block(row, t), block(row, t), sib))

    c_zr, c_hz, c_hx, c_hx2, c_hs = [], [], {}, {}, []
    own = []
    for t in range(2):
        zs[t] = collect(t, 0).astype(BF16)
        c_zr.append(rcopy(zs.at[t], zr.at[t], zpeer))
        own.append(collect(t, 1))
    lc_z, c_wx2, c_ws2 = weights_second()
    c_kvy2, c_ks = keys_second()
    residual(0, own[0])
    residual(1, own[1])
    for t in range(2):
        c_hz[t].wait_recv()
        c_hx2[t] = {d: rcopy(block(r_z, t), block(r_z, t), xpeer[d]) for d in (1, 2, 3)}
        c_hs.append(rcopy(block(r_z, t), block(r_z, t), sib))

    w_fwd = []
    for d in (1, 2, 3):
        src = at_row(zh, (x + 4 - d) % 4, k)
        c_wx[d].wait_recv()
        w_fwd.append(rcopy(wg.at[src], wg.at[src], sib))
        c_kvy[d].wait_recv()
        c_ks.append(rcopy(kb.at[k, d], kb.at[k, d], sib))
    for leg, cs in ((0, c_hx), (1, c_hx2)):
        for t in range(2):
            for d in (1, 2, 3):
                src = at_row(zh if leg == 0 else 1 - zh, (x + 4 - d) % 4, k)
                cs[t][d].wait_recv()
                c_hs.append(rcopy(block(src, t), block(src, t), sib))
    for d in (1, 2, 3):
        src = at_row(1 - zh, (x + 4 - d) % 4, k)
        c_wx2[d].wait_recv()
        w_fwd.append(rcopy(wg.at[src], wg.at[src], sib))

    c_kfwd = []
    for d in (1, 2, 3):
        c_kvy2[d].wait_recv()
        c_kfwd.append(rcopy(kb.at[k, 4 + d], kb.at[k, 4 + d], sib))

    lc_own.wait()
    lc_z.wait()
    for c in [c_ws, c_ws2, *w_fwd]:
        c.wait_recv()
    wfull = wg[...].reshape(D, 3 * GC)
    colsum = dot(wfull, jnp.ones((D, 128), BF16), 0, 0)
    for c in c_hs:
        c.wait_recv()

    hfull = hall[...].reshape(D, TOK)
    hf = hfull.astype(F32)
    mu = jnp.sum(hf, axis=0, keepdims=True) / D
    nvar = jnp.sum(hf * hf, axis=0, keepdims=True) / D - mu * mu
    rstd = lax.rsqrt(nvar + EPS)
    proj = dot(wfull, hfull, 0, 0)
    qkv = (proj - colsum[:, 0:1] * mu) * rstd
    qcm = (qkv[0:GC] * HEAD ** -0.5).astype(BF16)
    kf[0] = qkv[GC:2 * GC].astype(BF16)
    kf[1] = qkv[2 * GC:].astype(BF16)

    qi = lax.broadcasted_iota(jnp.int32, (QT, TOK), 0)
    ti = lax.broadcasted_iota(jnp.int32, (QT, TOK), 1)
    pick = (ti == (qi & 3) * ROWS + part * 32 + (qi >> 2)).astype(BF16)
    qtm = dot(pick, qcm, 1, 1).astype(BF16)
    qx[...] = qtm
    c_q = rcopy(qx, qpeer, qpartner)

    lc_kv.wait()
    for c in c_ks + c_kfwd:
        c.wait_recv()

    def head_rows(h):
        return pl.ds(h * HEAD, HEAD)

    def keys_of(h, own):
        first = kf[0, head_rows(h), :] if own else kb[0, 0, head_rows(h), :]
        return [first] + [kb[0, i, head_rows(h), :] for i in range(1, 8)]

    def values_of(h, own):
        first = kf[1, head_rows(h), :] if own else kb[1, 0, head_rows(h), :]
        return [first] + [kb[1, i, head_rows(h), :] for i in range(1, 8)]

    def weigh(scores, best, values):
        out = jnp.zeros((QT, HEAD + 16), F32)
        for s, v in zip(scores, values):
            p = jnp.exp(s - best).astype(BF16)
            out = out + dot(p, jnp.concatenate([v, jnp.ones((16, TOK), BF16)], axis=0), 1, 1)
        norm = out[:, HEAD:HEAD + 1]
        return out[:, 0:HEAD] / norm, best + jnp.log(norm)

    diag = lax.broadcasted_iota(jnp.int32, (QT, QT), 0) == lax.broadcasted_iota(jnp.int32, (QT, QT), 1)
    c_o = []

    def finish(h, own, scores, best):
        o, lse = weigh(scores, best, values_of(h, own))
        if own:
            oown[h] = o
            lses[h] = jnp.broadcast_to(lse, (QT, 128))
            return
        oret[h // 2, :, (h % 2) * HEAD:(h % 2 + 1) * HEAD] = o.astype(BF16)
        lret[h:h + 1] = jnp.sum(
            jnp.where(diag, jnp.broadcast_to(lse, (QT, QT)), 0.0), axis=0, keepdims=True
        )
        if h % 2 == 1:
            c_o.append(rcopy(oret.at[h // 2], oback.at[h // 2], qpartner))

    lret[...] = jnp.zeros((8, 128), F32)
    oret[2, :, HEAD:128] = jnp.zeros((QT, HEAD), BF16)
    held = None
    for own in (True, False):
        if not own:
            c_q.wait_recv()
        q_all = qtm if own else qpeer[...]
        for h in range(NHEAD):
            q = q_all[:, h * HEAD:(h + 1) * HEAD]
            scores = [dot(q, kk, 1, 0) for kk in keys_of(h, own)]
            top = scores[0]
            for sc in scores[1:]:
                top = jnp.maximum(top, sc)
            best = jnp.max(top, axis=1, keepdims=True)
            if held is not None:
                finish(*held)
            held = (h, own, scores, best)
    finish(*held)
    c_o.append(rcopy(oret.at[2], oback.at[2], qpartner))
    c_o.append(rcopy(lret, lback, qpartner))
    for c in c_o:
        c.wait_recv()

    outs = []
    for h in range(NHEAD):
        o1 = oback[h // 2, :, (h % 2) * HEAD:(h % 2 + 1) * HEAD].astype(F32)
        lse1 = as_column(lback[h:h + 1])
        lse0 = lses[h][:, 0:1]
        top = jnp.maximum(lse0, lse1)
        w0 = jnp.exp(lse0 - top)
        w1 = jnp.exp(lse1 - top)
        outs.append((oown[h] * w0 + o1 * w1) / (w0 + w1))
    attn_ref[...] = jnp.concatenate(outs, axis=1).astype(BF16)

    for c in started:
        c.wait_send()


def place(h_ref, a_ref, hid_ref, attn_ref):
    for w in range(COLS):
        hid_ref[:, w, :] = h_ref[:, w * ROWS:(w + 1) * ROWS]
    attn_ref[...] = a_ref[...].reshape(32, COLS, GC)


def on_device(latent, stale_act, stale_kv, gn_gain, gn_bias, temb, conv_w, w_qkv):
    group = lax.axis_index("row") // 4
    lat = latent.reshape(CH, TOK)
    edges = jnp.stack([stale_act[:, 0], stale_act[:, COLS - 1]])
    kv = lax.dynamic_slice_in_dim(stale_kv, group * GC, GC, 1).reshape(2, GC, TOK)
    vm = pl.BlockSpec(memory_space=pltpu.VMEM)
    hbm = pl.BlockSpec(memory_space=pl.ANY)
    scratch = [
        pltpu.VMEM((3, 240, D), BF16),
        pltpu.VMEM((HGROUPS, CH, 3 * GC), BF16),
        pltpu.VMEM((3, 2, 4, 2, CH, 240), BF16),
        pltpu.VMEM((3, 2, 4, CH, 240), BF16),
        pltpu.VMEM((240, 6 * ROWS), BF16),
        pltpu.VMEM((240, 6 * ROWS), BF16),
        pltpu.VMEM((2, CH, ROWS), BF16),
        pltpu.VMEM((8, 128), F32),
        pltpu.VMEM((15, 8, 128), F32),
        pltpu.VMEM((2, 2, 4, CH, HT), BF16),
        pltpu.VMEM((2, 2, 3, CH, HT), BF16),
        pltpu.VMEM((2, CH, HT), BF16),
        pltpu.VMEM((2, CH, HT), BF16),
        pltpu.VMEM((16, CH, TOK), BF16),
        pltpu.VMEM((2, CH, 3 * GC), BF16),
        pltpu.VMEM((16, CH, 3 * GC), BF16),
        pltpu.VMEM((2, 8, GC, TOK), BF16),
        pltpu.VMEM((2, GC, TOK), BF16),
        pltpu.VMEM((QT, GC), BF16),
        pltpu.VMEM((QT, GC), BF16),
        pltpu.VMEM((NHEAD, QT, HEAD), F32),
        pltpu.VMEM((3, QT, 128), BF16),
        pltpu.VMEM((3, QT, 128), BF16),
        pltpu.VMEM((8, 128), F32),
        pltpu.VMEM((8, 128), F32),
        pltpu.VMEM((NHEAD, QT, 128), F32),
        pltpu.SemaphoreType.DMA((NSEM,)),
        pltpu.SemaphoreType.DMA((NSEM,)),
        pltpu.SemaphoreType.DMA((4,)),
    ]
    hid, attn = pl.pallas_call(
        kernel,
        out_shape=(
            jax.ShapeDtypeStruct((CH, TOK), BF16),
            jax.ShapeDtypeStruct((QT, GC), BF16),
        ),
        in_specs=[vm, vm, hbm, vm, vm, vm, hbm, vm],
        out_specs=(vm, vm),
        scratch_shapes=scratch,
        compiler_params=pltpu.CompilerParams(
            collective_id=0, has_side_effects=True, vmem_limit_bytes=56 << 20
        ),
    )(
        lat, edges, kv, gn_gain.reshape(1, CH), gn_bias.reshape(1, CH), temb.reshape(1, CH),
        conv_w.reshape(3, 240, D), w_qkv.transpose(1, 0, 2),
    )
    return pl.pallas_call(
        place,
        out_shape=(
            jax.ShapeDtypeStruct((CH, COLS, ROWS), BF16),
            jax.ShapeDtypeStruct((32, COLS, GC), BF16),
        ),
        in_specs=[vm, vm],
        out_specs=(vm, vm),
    )(hid, attn)


def solution(mesh):
    return jax.shard_map(
        on_device,
        mesh=mesh,
        in_specs=(
            P("row", "col", None),
            P("row", "col", None),
            P(None, None, "col", None),
            P("row"),
            P("row"),
            P("row"),
            P(None, None, "row", None),
            P("row", None, None),
        ),
        out_specs=(P("row", "col", None), P("row", "col", None)),
        check_vma=False,
    )
```

```python
import itertools

import jax
import jax.numpy as jnp
from jax import lax
from jax.experimental import pallas as pl
from jax.experimental.pallas import tpu as pltpu
from jax.sharding import PartitionSpec as P

D = 1280
HEAD = 64
HGROUPS = 4
GROUPS = 32
EPS = 1e-05

F32 = jnp.float32
BF16 = jnp.bfloat16
MESH = pl.DeviceIdType.MESH

CH = 80
GC = 320
NHEAD = 5
COLS = 4
ROWS = 128
TOK = COLS * ROWS
QT = 128
NSEM = 128
HT = TOK // 2


def dot(a, b, ca, cb):
    return lax.dot_general(a, b, (((ca,), (cb,)), ((), ())), preferred_element_type=F32)


def as_column(row):
    n = row.shape[1]
    r = lax.broadcasted_iota(jnp.int32, (n, n), 0)
    c = lax.broadcasted_iota(jnp.int32, (n, n), 1)
    return jnp.sum(jnp.where(r == c, jnp.broadcast_to(row, (n, n)), 0.0), axis=1, keepdims=True)


def kernel(
    lat_ref, act_ref, kv_hbm, gain_ref, bias_ref, temb_ref, cw_hbm, w_ref,
    hid_ref, attn_ref,
    cw, edge, wsrc, wt, wtsib, x3, x3sib, halo, st_a, st_all, pb, rx, zs, zr,
    hall, wz, wg, kb, kf, qx, qpeer, oown, oret, oback, lret, lback, lses,
    ss, rs, ls,
):
    row = lax.axis_index("row")
    col = lax.axis_index("col")
    zh, x, k = row // 8, (row // 2) % 4, row % 2
    y, zl = col // 4, col % 4
    group = row // 4
    part = row % 4
    ids = itertools.count()

    def at_row(zh_, x_, k_):
        return zh_ * 8 + x_ * 2 + k_

    def dev(r, c):
        return (r, c)

    sib = dev(at_row(zh, x, 1 - k), col)
    wpeer = (at_row(1 - zh, x, k), y * 4 + 3 - zl)
    zpeer = dev(at_row(1 - zh, x, k), col)
    xs = {d: (x + d) % 4 for d in (1, 2, 3)}
    xpeer = {d: dev(at_row(zh, xs[d], k), col) for d in (1, 2, 3)}
    ypeer = {d: dev(row, ((y + d) % 4) * 4 + zl) for d in (1, 2, 3)}
    lpeer = {d: dev(row, y * 4 + (zl + d) % 4) for d in (1, 2, 3)}
    nxt = dev(row, (col + 1) % 16)
    prv = dev(row, (col + 15) % 16)
    flip = zl + 1 - 2 * (zl % 2)
    near = lpeer[2]
    qpartner = dev(row, y * 4 + flip)
    others = {
        (dy, dz): dev(row, ((y + dy) % 4) * 4 + (zl + dz) % 4)
        for dy in range(4) for dz in range(4) if dy or dz
    }
    r_z = at_row(1 - zh, x, k)

    started = []

    def rcopy(src, dst, to):
        i = next(ids)
        cp = pltpu.make_async_remote_copy(
            src_ref=src, dst_ref=dst, send_sem=ss.at[i], recv_sem=rs.at[i],
            device_id=to, device_id_type=MESH,
        )
        cp.start()
        started.append(cp)
        return cp

    lc_w = pltpu.make_async_copy(cw_hbm, cw, ls.at[0])
    lc_w.start()
    lc_kv = pltpu.make_async_copy(kv_hbm, kb.at[:, 0], ls.at[1])
    lc_kv.start()

    bar = pltpu.get_barrier_semaphore()
    peers = [sib, zpeer, wpeer, *xpeer.values(), *others.values(), nxt, prv]
    for p in peers:
        pl.semaphore_signal(bar, inc=1, device_id=p, device_id_type=MESH)

    for i in range(3):
        part_w = w_ref[i]
        for g in range(HGROUPS):
            wsrc[g, :, i * GC:(i + 1) * GC] = part_w[:, g * GC:(g + 1) * GC]
    lc_own = pltpu.make_async_copy(wsrc.at[group], wg.at[row], ls.at[2])
    lc_own.start()

    xf = jnp.concatenate([lat_ref[:, w, :].astype(F32) for w in range(COLS)], axis=1)
    n_loc = 40 * TOK
    halves = [xf[0:40], xf[40:80]]
    means = [jnp.sum(jnp.sum(h, axis=1, keepdims=True), axis=0, keepdims=True) / n_loc for h in halves]
    m2s = [
        jnp.sum(jnp.sum((h - m) * (h - m), axis=1, keepdims=True), axis=0, keepdims=True)
        for h, m in zip(halves, means)
    ]
    rid = lax.broadcasted_iota(jnp.int32, (8, 128), 0)
    tile = jnp.zeros((8, 128), F32)
    for i, v in enumerate(means + m2s):
        tile = jnp.where(rid == i, jnp.broadcast_to(v, (8, 128)), tile)
    st_a[...] = tile

    edge[0] = act_ref[:, 0, :]
    edge[1] = act_ref[:, COLS - 1, :]

    pl.semaphore_wait(bar, len(peers))

    c_st = [
        rcopy(st_a, st_all.at[dy * 4 + dz - 1], to) for (dy, dz), to in others.items()
    ]
    c_halo_n = rcopy(edge.at[1], halo.at[0], nxt)
    c_halo_p = rcopy(edge.at[0], halo.at[1], prv)

    c_wx = {d: rcopy(wsrc.at[zh * 2 + xs[d] // 2], wg.at[row], xpeer[d]) for d in (1, 2, 3)}
    c_ws = rcopy(wsrc.at[group], wg.at[row], sib)
    lc_w.wait()
    eye = (
        lax.broadcasted_iota(jnp.int32, (128, 128), 0) == lax.broadcasted_iota(jnp.int32, (128, 128), 1)
    ).astype(BF16)

    def flip_weights(a):
        for half in range(2):
            blocks = [
                dot(eye, cw[a, :, (half * 5 + i) * 128:(half * 5 + i + 1) * 128], 1, 1).astype(BF16)
                for i in range(5)
            ]
            wt[a, half] = jnp.concatenate(blocks, axis=0).reshape(4, 2, CH, 240)

    flip_weights(0)

    flip_weights(1)
    flip_weights(2)
    c_wt = rcopy(wt.at[:, :, :, 1 - k], wtsib, sib)

    lane = lax.broadcasted_iota(jnp.int32, (CH, ROWS), 1)

    def shifts(colv):
        left = jnp.where(lane == 0, 0.0, pltpu.roll(colv, 1, axis=1))
        right = jnp.where(lane == ROWS - 1, 0.0, pltpu.roll(colv, ROWS - 1, axis=1))
        return [left.astype(BF16), colv.astype(BF16), right.astype(BF16)]

    def put_column(slot, colv):
        for c, v in enumerate(shifts(colv)):
            x3[c * CH:(c + 1) * CH, slot * ROWS:(slot + 1) * ROWS] = v

    gain = as_column(gain_ref[...])
    bias = as_column(bias_ref[...])
    temb = as_column(temb_ref[...])

    c_halo_n.wait_recv()
    c_halo_p.wait_recv()
    put_column(0, jnp.where(col > 0, halo[0].astype(F32), 0.0))
    put_column(5, jnp.where(col < 15, halo[1].astype(F32), 0.0))

    for c in c_st:
        c.wait_recv()
    tiles = [tile] + [st_all[i] for i in range(15)]
    gmean = sum(t[0:2] for t in tiles) / 16.0
    gm2 = sum(t[2:4] for t in tiles)
    for t in tiles:
        dlt = t[0:2] - gmean
        gm2 = gm2 + float(n_loc) * dlt * dlt
    ginv = lax.rsqrt(gm2 / float(16 * n_loc) + EPS)
    c_wz = rcopy(wsrc.at[pl.ds(2 * (1 - zh), 2)], wz, wpeer)
    c_near = rcopy(kv_hbm.at[k], kb.at[k, 4], near)
    c_kvy = {d: rcopy(kv_hbm.at[k], kb.at[k, d], ypeer[d]) for d in (1, 2, 3)}
    mean_c = jnp.concatenate(
        [jnp.broadcast_to(gmean[0:1], (40, 128)), jnp.broadcast_to(gmean[1:2], (40, 128))], axis=0
    )
    inv_c = jnp.concatenate(
        [jnp.broadcast_to(ginv[0:1], (40, 128)), jnp.broadcast_to(ginv[1:2], (40, 128))], axis=0
    )
    for w in range(COLS):
        v = (xf[:, w * ROWS:(w + 1) * ROWS] - mean_c) * inv_c * gain + bias
        act = v / (1.0 + jnp.exp(-v))
        put_column(1 + w, act.astype(BF16).astype(F32))
    c_x3 = rcopy(x3, x3sib, sib)

    c_wt.wait_recv()
    c_x3.wait_recv()
    c_rx = {}
    for t in range(2):
        for half in range(2):
            zz = (1 - zh) if half == 0 else zh
            acc = jnp.zeros((4 * CH, HT), F32)
            for wv, xv in ((wt.at[:, :, :, k], x3), (wtsib, x3sib)):
                for a in range(3):
                    first = a * ROWS + t * HT
                    acc = acc + dot(
                        wv[a, zz].reshape(4 * CH, 240), xv[:, first:first + HT], 1, 0
                    )
            pb[t, half] = acc.astype(BF16).reshape(4, CH, HT)
            c_rx[t, half] = [
                rcopy(pb.at[t, half, xs[d]], rx.at[t, half, d - 1], xpeer[d]) for d in (1, 2, 3)
            ]

    def keys_second():
        c_near.wait_recv()
        ks = [rcopy(kb.at[k, 4], kb.at[k, 4], sib)]
        return {d: rcopy(kb.at[k, 4], kb.at[k, 4 + d], ypeer[d]) for d in (1, 2, 3)}, ks

    def weights_second():
        mine = x // 2
        c_wz.wait_recv()
        lc = pltpu.make_async_copy(wz.at[mine], wg.at[r_z], ls.at[3])
        lc.start()
        cx = {d: rcopy(wz.at[xs[d] // 2], wg.at[r_z], xpeer[d]) for d in (1, 2, 3)}
        return lc, cx, rcopy(wz.at[mine], wg.at[r_z], sib)

    def collect(t, half):
        total = pb[t, half, x].astype(F32)
        for d in range(3):
            c_rx[t, half][d].wait_recv()
            total = total + rx[t, half, d].astype(F32)
        return total

    def block(r, t):
        return hall.at[r, :, pl.ds(t * HT, HT)]

    def residual(t, own):
        c_zr[t].wait_recv()
        lanes = slice(t * HT, (t + 1) * HT)
        hid = (xf[:, lanes] + (own + zr[t].astype(F32)) + temb).astype(BF16)
        hid_ref[:, lanes] = hid
        hall[row, :, lanes] = hid
        c_hz.append(rcopy(block(row, t), block(row, t), zpeer))
        c_hx[t] = {d: rcopy(block(row, t), block(row, t), xpeer[d]) for d in (1, 2, 3)}
        c_hs.append(rcopy(block(row, t), block(row, t), sib))

    c_zr, c_hz, c_hx, c_hx2, c_hs = [], [], {}, {}, []
    own = []
    for t in range(2):
        zs[t] = collect(t, 0).astype(BF16)
        c_zr.append(rcopy(zs.at[t], zr.at[t], zpeer))
        own.append(collect(t, 1))
    lc_z, c_wx2, c_ws2 = weights_second()
    c_kvy2, c_ks = keys_second()
    residual(0, own[0])
    residual(1, own[1])
    for t in range(2):
        c_hz[t].wait_recv()
        c_hx2[t] = {d: rcopy(block(r_z, t), block(r_z, t), xpeer[d]) for d in (1, 2, 3)}
        c_hs.append(rcopy(block(r_z, t), block(r_z, t), sib))

    w_fwd = []
    for d in (1, 2, 3):
        src = at_row(zh, (x + 4 - d) % 4, k)
        c_wx[d].wait_recv()
        w_fwd.append(rcopy(wg.at[src], wg.at[src], sib))
        c_kvy[d].wait_recv()
        c_ks.append(rcopy(kb.at[k, d], kb.at[k, d], sib))
    for leg, cs in ((0, c_hx), (1, c_hx2)):
        for t in range(2):
            for d in (1, 2, 3):
                src = at_row(zh if leg == 0 else 1 - zh, (x + 4 - d) % 4, k)
                cs[t][d].wait_recv()
                c_hs.append(rcopy(block(src, t), block(src, t), sib))
    for d in (1, 2, 3):
        src = at_row(1 - zh, (x + 4 - d) % 4, k)
        c_wx2[d].wait_recv()
        w_fwd.append(rcopy(wg.at[src], wg.at[src], sib))

    c_kfwd = []
    for d in (1, 2, 3):
        c_kvy2[d].wait_recv()
        c_kfwd.append(rcopy(kb.at[k, 4 + d], kb.at[k, 4 + d], sib))

    lc_own.wait()
    lc_z.wait()
    for c in [c_ws, c_ws2, *w_fwd]:
        c.wait_recv()
    wfull = wg[...].reshape(D, 3 * GC)
    colsum = dot(wfull, jnp.ones((D, 128), BF16), 0, 0)
    for c in c_hs:
        c.wait_recv()

    hfull = hall[...].reshape(D, TOK)
    hf = hfull.astype(F32)
    mu = jnp.sum(hf, axis=0, keepdims=True) / D
    nvar = jnp.sum(hf * hf, axis=0, keepdims=True) / D - mu * mu
    rstd = lax.rsqrt(nvar + EPS)
    proj = dot(wfull, hfull, 0, 0)
    qkv = (proj - colsum[:, 0:1] * mu) * rstd
    qcm = (qkv[0:GC] * HEAD ** -0.5).astype(BF16)
    kf[0] = qkv[GC:2 * GC].astype(BF16)
    kf[1] = qkv[2 * GC:].astype(BF16)

    qi = lax.broadcasted_iota(jnp.int32, (QT, TOK), 0)
    ti = lax.broadcasted_iota(jnp.int32, (QT, TOK), 1)
    pick = (ti == (qi & 3) * ROWS + part * 32 + (qi >> 2)).astype(BF16)
    qtm = dot(pick, qcm, 1, 1).astype(BF16)
    qx[...] = qtm
    c_q = rcopy(qx, qpeer, qpartner)

    lc_kv.wait()
    for c in c_ks + c_kfwd:
        c.wait_recv()

    def head_rows(h):
        return pl.ds(h * HEAD, HEAD)

    def keys_of(h, own):
        first = kf[0, head_rows(h), :] if own else kb[0, 0, head_rows(h), :]
        return [first] + [kb[0, i, head_rows(h), :] for i in range(1, 8)]

    def values_of(h, own):
        first = kf[1, head_rows(h), :] if own else kb[1, 0, head_rows(h), :]
        return [first] + [kb[1, i, head_rows(h), :] for i in range(1, 8)]

    def weigh(scores, best, values):
        out = jnp.zeros((QT, HEAD + 16), F32)
        for s, v in zip(scores, values):
            p = jnp.exp(s - best).astype(BF16)
            out = out + dot(p, jnp.concatenate([v, jnp.ones((16, TOK), BF16)], axis=0), 1, 1)
        norm = out[:, HEAD:HEAD + 1]
        return out[:, 0:HEAD] / norm, best + jnp.log(norm)

    diag = lax.broadcasted_iota(jnp.int32, (QT, QT), 0) == lax.broadcasted_iota(jnp.int32, (QT, QT), 1)
    c_o = []

    def finish(h, own, scores, best):
        o, lse = weigh(scores, best, values_of(h, own))
        if own:
            oown[h] = o
            lses[h] = jnp.broadcast_to(lse, (QT, 128))
            return
        oret[h // 2, :, (h % 2) * HEAD:(h % 2 + 1) * HEAD] = o.astype(BF16)
        lret[h:h + 1] = jnp.sum(
            jnp.where(diag, jnp.broadcast_to(lse, (QT, QT)), 0.0), axis=0, keepdims=True
        )
        if h % 2 == 1:
            c_o.append(rcopy(oret.at[h // 2], oback.at[h // 2], qpartner))

    lret[...] = jnp.zeros((8, 128), F32)
    oret[2, :, HEAD:128] = jnp.zeros((QT, HEAD), BF16)
    held = None
    for own in (True, False):
        if not own:
            c_q.wait_recv()
        q_all = qtm if own else qpeer[...]
        for h in range(NHEAD):
            q = q_all[:, h * HEAD:(h + 1) * HEAD]
            scores = [dot(q, kk, 1, 0) for kk in keys_of(h, own)]
            top = scores[0]
            for sc in scores[1:]:
                top = jnp.maximum(top, sc)
            best = jnp.max(top, axis=1, keepdims=True)
            if held is not None:
                finish(*held)
            held = (h, own, scores, best)
    finish(*held)
    c_o.append(rcopy(oret.at[2], oback.at[2], qpartner))
    c_o.append(rcopy(lret, lback, qpartner))
    for c in c_o:
        c.wait_recv()

    outs = []
    for h in range(NHEAD):
        o1 = oback[h // 2, :, (h % 2) * HEAD:(h % 2 + 1) * HEAD].astype(F32)
        lse1 = as_column(lback[h:h + 1])
        lse0 = lses[h][:, 0:1]
        top = jnp.maximum(lse0, lse1)
        w0 = jnp.exp(lse0 - top)
        w1 = jnp.exp(lse1 - top)
        outs.append((oown[h] * w0 + o1 * w1) / (w0 + w1))
    attn_ref[...] = jnp.concatenate(outs, axis=1).astype(BF16)

    for c in started:
        c.wait_send()


def place(h_ref, a_ref, hid_ref, attn_ref):
    for w in range(COLS):
        hid_ref[:, w, :] = h_ref[:, w * ROWS:(w + 1) * ROWS]
    attn_ref[...] = a_ref[...].reshape(32, COLS, GC)


def on_device(latent, stale_act, stale_kv, gn_gain, gn_bias, temb, conv_w, w_qkv):
    group = lax.axis_index("row") // 4
    kv = lax.dynamic_slice_in_dim(stale_kv, group * GC, GC, 1).reshape(2, GC, TOK)
    vm = pl.BlockSpec(memory_space=pltpu.VMEM)
    hbm = pl.BlockSpec(memory_space=pl.ANY)
    scratch = [
        pltpu.VMEM((3, 240, D), BF16),
        pltpu.VMEM((2, CH, ROWS), BF16),
        pltpu.VMEM((HGROUPS, CH, 3 * GC), BF16),
        pltpu.VMEM((3, 2, 4, 2, CH, 240), BF16),
        pltpu.VMEM((3, 2, 4, CH, 240), BF16),
        pltpu.VMEM((240, 6 * ROWS), BF16),
        pltpu.VMEM((240, 6 * ROWS), BF16),
        pltpu.VMEM((2, CH, ROWS), BF16),
        pltpu.VMEM((8, 128), F32),
        pltpu.VMEM((15, 8, 128), F32),
        pltpu.VMEM((2, 2, 4, CH, HT), BF16),
        pltpu.VMEM((2, 2, 3, CH, HT), BF16),
        pltpu.VMEM((2, CH, HT), BF16),
        pltpu.VMEM((2, CH, HT), BF16),
        pltpu.VMEM((16, CH, TOK), BF16),
        pltpu.VMEM((2, CH, 3 * GC), BF16),
        pltpu.VMEM((16, CH, 3 * GC), BF16),
        pltpu.VMEM((2, 8, GC, TOK), BF16),
        pltpu.VMEM((2, GC, TOK), BF16),
        pltpu.VMEM((QT, GC), BF16),
        pltpu.VMEM((QT, GC), BF16),
        pltpu.VMEM((NHEAD, QT, HEAD), F32),
        pltpu.VMEM((3, QT, 128), BF16),
        pltpu.VMEM((3, QT, 128), BF16),
        pltpu.VMEM((8, 128), F32),
        pltpu.VMEM((8, 128), F32),
        pltpu.VMEM((NHEAD, QT, 128), F32),
        pltpu.SemaphoreType.DMA((NSEM,)),
        pltpu.SemaphoreType.DMA((NSEM,)),
        pltpu.SemaphoreType.DMA((4,)),
    ]
    hid, attn = pl.pallas_call(
        kernel,
        out_shape=(
            jax.ShapeDtypeStruct((CH, TOK), BF16),
            jax.ShapeDtypeStruct((QT, GC), BF16),
        ),
        in_specs=[vm, vm, hbm, vm, vm, vm, hbm, vm],
        out_specs=(vm, vm),
        scratch_shapes=scratch,
        compiler_params=pltpu.CompilerParams(
            collective_id=0, has_side_effects=True, vmem_limit_bytes=56 << 20
        ),
    )(
        latent, stale_act, kv, gn_gain.reshape(1, CH), gn_bias.reshape(1, CH), temb.reshape(1, CH),
        conv_w.reshape(3, 240, D), w_qkv.transpose(1, 0, 2),
    )
    return pl.pallas_call(
        place,
        out_shape=(
            jax.ShapeDtypeStruct((CH, COLS, ROWS), BF16),
            jax.ShapeDtypeStruct((32, COLS, GC), BF16),
        ),
        in_specs=[vm, vm],
        out_specs=(vm, vm),
    )(hid, attn)


def solution(mesh):
    return jax.shard_map(
        on_device,
        mesh=mesh,
        in_specs=(
            P("row", "col", None),
            P("row", "col", None),
            P(None, None, "col", None),
            P("row"),
            P("row"),
            P("row"),
            P(None, None, "row", None),
            P("row", None, None),
        ),
        out_specs=(P("row", "col", None), P("row", "col", None)),
        check_vma=False,
    )
```

```python
import itertools

import jax
import jax.numpy as jnp
from jax import lax
from jax.experimental import pallas as pl
from jax.experimental.pallas import tpu as pltpu
from jax.sharding import PartitionSpec as P

D = 1280
HEAD = 64
HGROUPS = 4
GROUPS = 32
EPS = 1e-05

F32 = jnp.float32
BF16 = jnp.bfloat16
MESH = pl.DeviceIdType.MESH

CH = 80
GC = 320
NHEAD = 5
COLS = 4
ROWS = 128
TOK = COLS * ROWS
QT = 128
NSEM = 128
HT = TOK // 2


def dot(a, b, ca, cb):
    return lax.dot_general(a, b, (((ca,), (cb,)), ((), ())), preferred_element_type=F32)


def as_column(row):
    n = row.shape[1]
    r = lax.broadcasted_iota(jnp.int32, (n, n), 0)
    c = lax.broadcasted_iota(jnp.int32, (n, n), 1)
    return jnp.sum(jnp.where(r == c, jnp.broadcast_to(row, (n, n)), 0.0), axis=1, keepdims=True)


def kernel(
    lat_ref, act_ref, kv_hbm, gain_ref, bias_ref, temb_ref, cw_hbm, w_ref,
    hid_ref, attn_ref,
    cw, edge, wsrc, wt, wtsib, x3, x3sib, halo, st_a, st_all, pb, rx, zs, zr,
    hall, wz, wg, kb, kf, qx, qpeer, oown, oret, oback, lret, lback, lses,
    ss, rs, ls,
):
    row = lax.axis_index("row")
    col = lax.axis_index("col")
    zh, x, k = row // 8, (row // 2) % 4, row % 2
    y, zl = col // 4, col % 4
    group = row // 4
    part = row % 4
    ids = itertools.count()

    def at_row(zh_, x_, k_):
        return zh_ * 8 + x_ * 2 + k_

    def dev(r, c):
        return (r, c)

    sib = dev(at_row(zh, x, 1 - k), col)
    wpeer = (at_row(1 - zh, x, k), y * 4 + 3 - zl)
    zpeer = dev(at_row(1 - zh, x, k), col)
    xs = {d: (x + d) % 4 for d in (1, 2, 3)}
    xpeer = {d: dev(at_row(zh, xs[d], k), col) for d in (1, 2, 3)}
    ypeer = {d: dev(row, ((y + d) % 4) * 4 + zl) for d in (1, 2, 3)}
    lpeer = {d: dev(row, y * 4 + (zl + d) % 4) for d in (1, 2, 3)}
    nxt = dev(row, (col + 1) % 16)
    prv = dev(row, (col + 15) % 16)
    flip = zl + 1 - 2 * (zl % 2)
    near = lpeer[2]
    qpartner = dev(row, y * 4 + flip)
    others = {
        (dy, dz): dev(row, ((y + dy) % 4) * 4 + (zl + dz) % 4)
        for dy in range(4) for dz in range(4) if dy or dz
    }
    r_z = at_row(1 - zh, x, k)

    started = []

    def rcopy(src, dst, to):
        i = next(ids)
        cp = pltpu.make_async_remote_copy(
            src_ref=src, dst_ref=dst, send_sem=ss.at[i], recv_sem=rs.at[i],
            device_id=to, device_id_type=MESH,
        )
        cp.start()
        started.append(cp)
        return cp

    lc_w = pltpu.make_async_copy(cw_hbm, cw, ls.at[0])
    lc_w.start()
    lc_kv = pltpu.make_async_copy(kv_hbm, kb.at[:, 0], ls.at[1])
    lc_kv.start()

    bar = pltpu.get_barrier_semaphore()
    peers = [sib, zpeer, wpeer, *xpeer.values(), *others.values(), nxt, prv]
    for p in peers:
        pl.semaphore_signal(bar, inc=1, device_id=p, device_id_type=MESH)

    for i in range(3):
        part_w = w_ref[i]
        for g in range(HGROUPS):
            wsrc[g, :, i * GC:(i + 1) * GC] = part_w[:, g * GC:(g + 1) * GC]
    lc_own = pltpu.make_async_copy(wsrc.at[group], wg.at[row], ls.at[2])
    lc_own.start()

    xf = jnp.concatenate([lat_ref[:, w, :].astype(F32) for w in range(COLS)], axis=1)
    n_loc = 40 * TOK
    halves = [xf[0:40], xf[40:80]]
    means = [jnp.sum(jnp.sum(h, axis=1, keepdims=True), axis=0, keepdims=True) / n_loc for h in halves]
    m2s = [
        jnp.sum(jnp.sum((h - m) * (h - m), axis=1, keepdims=True), axis=0, keepdims=True)
        for h, m in zip(halves, means)
    ]
    rid = lax.broadcasted_iota(jnp.int32, (8, 128), 0)
    tile = jnp.zeros((8, 128), F32)
    for i, v in enumerate(means + m2s):
        tile = jnp.where(rid == i, jnp.broadcast_to(v, (8, 128)), tile)
    st_a[...] = tile

    edge[0] = act_ref[:, 0, :]
    edge[1] = act_ref[:, COLS - 1, :]

    pl.semaphore_wait(bar, len(peers))

    c_st = [
        rcopy(st_a, st_all.at[dy * 4 + dz - 1], to) for (dy, dz), to in others.items()
    ]
    c_halo_n = rcopy(edge.at[1], halo.at[0], nxt)
    c_halo_p = rcopy(edge.at[0], halo.at[1], prv)

    c_wx = {d: rcopy(wsrc.at[zh * 2 + xs[d] // 2], wg.at[row], xpeer[d]) for d in (1, 2, 3)}
    c_ws = rcopy(wsrc.at[group], wg.at[row], sib)
    lc_w.wait()
    eye = (
        lax.broadcasted_iota(jnp.int32, (128, 128), 0) == lax.broadcasted_iota(jnp.int32, (128, 128), 1)
    ).astype(BF16)

    def flip_weights(a):
        for half in range(2):
            blocks = [
                dot(eye, cw[a, :, (half * 5 + i) * 128:(half * 5 + i + 1) * 128], 1, 1).astype(BF16)
                for i in range(5)
            ]
            wt[a, half] = jnp.concatenate(blocks, axis=0).reshape(4, 2, CH, 240)

    flip_weights(0)

    flip_weights(1)
    flip_weights(2)
    c_wt = rcopy(wt.at[:, :, :, 1 - k], wtsib, sib)

    lane = lax.broadcasted_iota(jnp.int32, (CH, ROWS), 1)

    def shifts(colv):
        left = jnp.where(lane == 0, 0.0, pltpu.roll(colv, 1, axis=1))
        right = jnp.where(lane == ROWS - 1, 0.0, pltpu.roll(colv, ROWS - 1, axis=1))
        return [left.astype(BF16), colv.astype(BF16), right.astype(BF16)]

    def put_column(slot, colv):
        for c, v in enumerate(shifts(colv)):
            x3[c * CH:(c + 1) * CH, slot * ROWS:(slot + 1) * ROWS] = v

    gain = as_column(gain_ref[...])
    bias = as_column(bias_ref[...])
    temb = as_column(temb_ref[...])

    c_halo_n.wait_recv()
    c_halo_p.wait_recv()
    put_column(0, jnp.where(col > 0, halo[0].astype(F32), 0.0))
    put_column(5, jnp.where(col < 15, halo[1].astype(F32), 0.0))

    for c in c_st:
        c.wait_recv()
    tiles = [tile] + [st_all[i] for i in range(15)]
    gmean = sum(t[0:2] for t in tiles) / 16.0
    gm2 = sum(t[2:4] for t in tiles)
    for t in tiles:
        dlt = t[0:2] - gmean
        gm2 = gm2 + float(n_loc) * dlt * dlt
    ginv = lax.rsqrt(gm2 / float(16 * n_loc) + EPS)
    c_wz = rcopy(wsrc.at[pl.ds(2 * (1 - zh), 2)], wz, wpeer)
    c_near = rcopy(kv_hbm.at[k], kb.at[k, 4], near)
    c_kvy = {d: rcopy(kv_hbm.at[k], kb.at[k, d], ypeer[d]) for d in (1, 2, 3)}
    mean_c = jnp.concatenate(
        [jnp.broadcast_to(gmean[0:1], (40, 128)), jnp.broadcast_to(gmean[1:2], (40, 128))], axis=0
    )
    inv_c = jnp.concatenate(
        [jnp.broadcast_to(ginv[0:1], (40, 128)), jnp.broadcast_to(ginv[1:2], (40, 128))], axis=0
    )
    for w in range(COLS):
        v = (xf[:, w * ROWS:(w + 1) * ROWS] - mean_c) * inv_c * gain + bias
        act = v / (1.0 + jnp.exp(-v))
        put_column(1 + w, act.astype(BF16).astype(F32))
    c_x3 = rcopy(x3, x3sib, sib)

    c_wt.wait_recv()
    c_x3.wait_recv()
    c_rx = {}
    for t in range(2):
        for half in range(2):
            zz = (1 - zh) if half == 0 else zh
            acc = jnp.zeros((4 * CH, HT), F32)
            for wv, xv in ((wt.at[:, :, :, k], x3), (wtsib, x3sib)):
                for a in range(3):
                    first = a * ROWS + t * HT
                    acc = acc + dot(
                        wv[a, zz].reshape(4 * CH, 240), xv[:, first:first + HT], 1, 0
                    )
            pb[t, half] = acc.astype(BF16).reshape(4, CH, HT)
            c_rx[t, half] = [
                rcopy(pb.at[t, half, xs[d]], rx.at[t, half, d - 1], xpeer[d]) for d in (1, 2, 3)
            ]

    def keys_second():
        c_near.wait_recv()
        ks = [rcopy(kb.at[k, 4], kb.at[k, 4], sib)]
        return {d: rcopy(kb.at[k, 4], kb.at[k, 4 + d], ypeer[d]) for d in (1, 2, 3)}, ks

    def weights_second():
        mine = x // 2
        c_wz.wait_recv()
        lc = pltpu.make_async_copy(wz.at[mine], wg.at[r_z], ls.at[3])
        lc.start()
        cx = {d: rcopy(wz.at[xs[d] // 2], wg.at[r_z], xpeer[d]) for d in (1, 2, 3)}
        return lc, cx, rcopy(wz.at[mine], wg.at[r_z], sib)

    def collect(t, half):
        total = pb[t, half, x].astype(F32)
        for d in range(3):
            c_rx[t, half][d].wait_recv()
            total = total + rx[t, half, d].astype(F32)
        return total

    def block(r, t):
        return hall.at[r, :, pl.ds(t * HT, HT)]

    def residual(t, own):
        c_zr[t].wait_recv()
        lanes = slice(t * HT, (t + 1) * HT)
        hid = (xf[:, lanes] + (own + zr[t].astype(F32)) + temb).astype(BF16)
        hid_ref[:, lanes] = hid
        hall[row, :, lanes] = hid
        c_hz.append(rcopy(block(row, t), block(row, t), zpeer))
        c_hx[t] = {d: rcopy(block(row, t), block(row, t), xpeer[d]) for d in (1, 2, 3)}
        c_hs.append(rcopy(block(row, t), block(row, t), sib))

    c_zr, c_hz, c_hx, c_hx2, c_hs = [], [], {}, {}, []
    own = []
    for t in range(2):
        zs[t] = collect(t, 0).astype(BF16)
        c_zr.append(rcopy(zs.at[t], zr.at[t], zpeer))
        own.append(collect(t, 1))
    lc_z, c_wx2, c_ws2 = weights_second()
    c_kvy2, c_ks = keys_second()
    residual(0, own[0])
    residual(1, own[1])
    for t in range(2):
        c_hz[t].wait_recv()
        c_hx2[t] = {d: rcopy(block(r_z, t), block(r_z, t), xpeer[d]) for d in (1, 2, 3)}
        c_hs.append(rcopy(block(r_z, t), block(r_z, t), sib))

    w_fwd = []
    for d in (1, 2, 3):
        src = at_row(zh, (x + 4 - d) % 4, k)
        c_wx[d].wait_recv()
        w_fwd.append(rcopy(wg.at[src], wg.at[src], sib))
        c_kvy[d].wait_recv()
        c_ks.append(rcopy(kb.at[k, d], kb.at[k, d], sib))
    for leg, cs in ((0, c_hx), (1, c_hx2)):
        for t in range(2):
            for d in (1, 2, 3):
                src = at_row(zh if leg == 0 else 1 - zh, (x + 4 - d) % 4, k)
                cs[t][d].wait_recv()
                c_hs.append(rcopy(block(src, t), block(src, t), sib))
    for d in (1, 2, 3):
        src = at_row(1 - zh, (x + 4 - d) % 4, k)
        c_wx2[d].wait_recv()
        w_fwd.append(rcopy(wg.at[src], wg.at[src], sib))


    lc_own.wait()
    lc_z.wait()
    for c in [c_ws, c_ws2, *w_fwd]:
        c.wait_recv()
    wfull = wg[...].reshape(D, 3 * GC)
    colsum = dot(wfull, jnp.ones((D, 128), BF16), 0, 0)
    for c in c_hs:
        c.wait_recv()

    c_kfwd = []
    for d in (1, 2, 3):
        c_kvy2[d].wait_recv()
        c_kfwd.append(rcopy(kb.at[k, 4 + d], kb.at[k, 4 + d], sib))

    hfull = hall[...].reshape(D, TOK)
    hf = hfull.astype(F32)
    mu = jnp.sum(hf, axis=0, keepdims=True) / D
    nvar = jnp.sum(hf * hf, axis=0, keepdims=True) / D - mu * mu
    rstd = lax.rsqrt(nvar + EPS)
    proj = dot(wfull, hfull, 0, 0)
    qkv = (proj - colsum[:, 0:1] * mu) * rstd
    qcm = (qkv[0:GC] * HEAD ** -0.5).astype(BF16)
    kf[0] = qkv[GC:2 * GC].astype(BF16)
    kf[1] = qkv[2 * GC:].astype(BF16)

    qi = lax.broadcasted_iota(jnp.int32, (QT, TOK), 0)
    ti = lax.broadcasted_iota(jnp.int32, (QT, TOK), 1)
    pick = (ti == (qi & 3) * ROWS + part * 32 + (qi >> 2)).astype(BF16)
    qtm = dot(pick, qcm, 1, 1).astype(BF16)
    qx[...] = qtm
    c_q = rcopy(qx, qpeer, qpartner)

    lc_kv.wait()
    for c in c_ks + c_kfwd:
        c.wait_recv()

    def head_rows(h):
        return pl.ds(h * HEAD, HEAD)

    def keys_of(h, own):
        first = kf[0, head_rows(h), :] if own else kb[0, 0, head_rows(h), :]
        return [first] + [kb[0, i, head_rows(h), :] for i in range(1, 8)]

    def values_of(h, own):
        first = kf[1, head_rows(h), :] if own else kb[1, 0, head_rows(h), :]
        return [first] + [kb[1, i, head_rows(h), :] for i in range(1, 8)]

    def weigh(scores, best, values):
        out = jnp.zeros((QT, HEAD + 16), F32)
        for s, v in zip(scores, values):
            p = jnp.exp(s - best).astype(BF16)
            out = out + dot(p, jnp.concatenate([v, jnp.ones((16, TOK), BF16)], axis=0), 1, 1)
        norm = out[:, HEAD:HEAD + 1]
        return out[:, 0:HEAD] / norm, best + jnp.log(norm)

    diag = lax.broadcasted_iota(jnp.int32, (QT, QT), 0) == lax.broadcasted_iota(jnp.int32, (QT, QT), 1)
    c_o = []

    def finish(h, own, scores, best):
        o, lse = weigh(scores, best, values_of(h, own))
        if own:
            oown[h] = o
            lses[h] = jnp.broadcast_to(lse, (QT, 128))
            return
        oret[h // 2, :, (h % 2) * HEAD:(h % 2 + 1) * HEAD] = o.astype(BF16)
        lret[h:h + 1] = jnp.sum(
            jnp.where(diag, jnp.broadcast_to(lse, (QT, QT)), 0.0), axis=0, keepdims=True
        )
        if h % 2 == 1:
            c_o.append(rcopy(oret.at[h // 2], oback.at[h // 2], qpartner))

    lret[...] = jnp.zeros((8, 128), F32)
    oret[2, :, HEAD:128] = jnp.zeros((QT, HEAD), BF16)
    held = None
    for own in (True, False):
        if not own:
            c_q.wait_recv()
        q_all = qtm if own else qpeer[...]
        for h in range(NHEAD):
            q = q_all[:, h * HEAD:(h + 1) * HEAD]
            scores = [dot(q, kk, 1, 0) for kk in keys_of(h, own)]
            top = scores[0]
            for sc in scores[1:]:
                top = jnp.maximum(top, sc)
            best = jnp.max(top, axis=1, keepdims=True)
            if held is not None:
                finish(*held)
            held = (h, own, scores, best)
    finish(*held)
    c_o.append(rcopy(oret.at[2], oback.at[2], qpartner))
    c_o.append(rcopy(lret, lback, qpartner))
    for c in c_o:
        c.wait_recv()

    outs = []
    for h in range(NHEAD):
        o1 = oback[h // 2, :, (h % 2) * HEAD:(h % 2 + 1) * HEAD].astype(F32)
        lse1 = as_column(lback[h:h + 1])
        lse0 = lses[h][:, 0:1]
        top = jnp.maximum(lse0, lse1)
        w0 = jnp.exp(lse0 - top)
        w1 = jnp.exp(lse1 - top)
        outs.append((oown[h] * w0 + o1 * w1) / (w0 + w1))
    attn_ref[...] = jnp.concatenate(outs, axis=1).astype(BF16)

    for c in started:
        c.wait_send()


def place(h_ref, a_ref, hid_ref, attn_ref):
    for w in range(COLS):
        hid_ref[:, w, :] = h_ref[:, w * ROWS:(w + 1) * ROWS]
    attn_ref[...] = a_ref[...].reshape(32, COLS, GC)


def on_device(latent, stale_act, stale_kv, gn_gain, gn_bias, temb, conv_w, w_qkv):
    group = lax.axis_index("row") // 4
    kv = lax.dynamic_slice_in_dim(stale_kv, group * GC, GC, 1).reshape(2, GC, TOK)
    vm = pl.BlockSpec(memory_space=pltpu.VMEM)
    hbm = pl.BlockSpec(memory_space=pl.ANY)
    scratch = [
        pltpu.VMEM((3, 240, D), BF16),
        pltpu.VMEM((2, CH, ROWS), BF16),
        pltpu.VMEM((HGROUPS, CH, 3 * GC), BF16),
        pltpu.VMEM((3, 2, 4, 2, CH, 240), BF16),
        pltpu.VMEM((3, 2, 4, CH, 240), BF16),
        pltpu.VMEM((240, 6 * ROWS), BF16),
        pltpu.VMEM((240, 6 * ROWS), BF16),
        pltpu.VMEM((2, CH, ROWS), BF16),
        pltpu.VMEM((8, 128), F32),
        pltpu.VMEM((15, 8, 128), F32),
        pltpu.VMEM((2, 2, 4, CH, HT), BF16),
        pltpu.VMEM((2, 2, 3, CH, HT), BF16),
        pltpu.VMEM((2, CH, HT), BF16),
        pltpu.VMEM((2, CH, HT), BF16),
        pltpu.VMEM((16, CH, TOK), BF16),
        pltpu.VMEM((2, CH, 3 * GC), BF16),
        pltpu.VMEM((16, CH, 3 * GC), BF16),
        pltpu.VMEM((2, 8, GC, TOK), BF16),
        pltpu.VMEM((2, GC, TOK), BF16),
        pltpu.VMEM((QT, GC), BF16),
        pltpu.VMEM((QT, GC), BF16),
        pltpu.VMEM((NHEAD, QT, HEAD), F32),
        pltpu.VMEM((3, QT, 128), BF16),
        pltpu.VMEM((3, QT, 128), BF16),
        pltpu.VMEM((8, 128), F32),
        pltpu.VMEM((8, 128), F32),
        pltpu.VMEM((NHEAD, QT, 128), F32),
        pltpu.SemaphoreType.DMA((NSEM,)),
        pltpu.SemaphoreType.DMA((NSEM,)),
        pltpu.SemaphoreType.DMA((4,)),
    ]
    hid, attn = pl.pallas_call(
        kernel,
        out_shape=(
            jax.ShapeDtypeStruct((CH, TOK), BF16),
            jax.ShapeDtypeStruct((QT, GC), BF16),
        ),
        in_specs=[vm, vm, hbm, vm, vm, vm, hbm, vm],
        out_specs=(vm, vm),
        scratch_shapes=scratch,
        compiler_params=pltpu.CompilerParams(
            collective_id=0, has_side_effects=True, vmem_limit_bytes=56 << 20
        ),
    )(
        latent, stale_act, kv, gn_gain.reshape(1, CH), gn_bias.reshape(1, CH), temb.reshape(1, CH),
        conv_w.reshape(3, 240, D), w_qkv.transpose(1, 0, 2),
    )
    return pl.pallas_call(
        place,
        out_shape=(
            jax.ShapeDtypeStruct((CH, COLS, ROWS), BF16),
            jax.ShapeDtypeStruct((32, COLS, GC), BF16),
        ),
        in_specs=[vm, vm],
        out_specs=(vm, vm),
    )(hid, attn)


def solution(mesh):
    return jax.shard_map(
        on_device,
        mesh=mesh,
        in_specs=(
            P("row", "col", None),
            P("row", "col", None),
            P(None, None, "col", None),
            P("row"),
            P("row"),
            P("row"),
            P(None, None, "row", None),
            P("row", None, None),
        ),
        out_specs=(P("row", "col", None), P("row", "col", None)),
        check_vma=False,
    )
```
